128 devices in a mesh: gx: 16 (over z, x), gy: 8 (over y, core).
Axes of the slice: x: 4, y: 4, z: 4, core: 2. Of those that a mesh axis runs over, the one named last changes fastest.
Arguments:
- fields: float32 [6, 1024, 64, 1024], P(None, 'gx', 'gy'), may hold values from -2 to 2, as said below
- owner: int32 [32, 64], P('gx', 'gy'), may hold values from 0 to 15, as said below
Outputs:
- owned: float32 [8, 256, 6, 32, 1024], P('gy', 'gx')
- owned_id: int32 [8, 256], P('gy', 'gx')
The draws below stay inside these ranges and needn't reach their ends.
Inputs may be any that keep to these rules, and one draw needn't show every extreme that they name: fields[0] (density) and fields[4] (pressure) lie in 0.5 to 2, fields[1] to fields[3] in -2 to 2, fields[5] in 0 to 1. Grids with x index a and y index b go to the device with gx index owner[a, b] and gy index b // 8; the grids of one device go to distinct owners, one to each gx index, so every device owns exactly 16 grids.
All inputs are finite; a program needn't handle non-finite values.
Results may differ from the reference program's by a relative error of at most 0.0003.
Values sent between devices are 32-bit elements; how exact they have to be, the bound alone decides.
A program may use at most 256 MiB of HBM per device.

```python
import jax
import jax.numpy as jnp
from jax import lax

CELLS = 32
FIELDS = 6
GPX = 2
GPY = 8
PLANE = 1024
GXT = 32
NYG = 64
NX = 1024
N_GX = 16
N_GY = 8


def draw_fields(key, part):
    key = jax.random.fold_in(key, 5)
    subkeys = jax.random.split(key, 4)
    shape = (NX, NYG, PLANE)
    density = jnp.exp(jax.random.uniform(subkeys[0], shape, jnp.float32, -0.65, 0.65))
    motion = jnp.clip(0.6 * jax.random.normal(subkeys[1], (3,) + shape, jnp.float32), -2.0, 2.0)
    pressure = jnp.exp(jax.random.uniform(subkeys[2], shape, jnp.float32, -0.65, 0.65))
    metals = jax.random.uniform(subkeys[3], shape, jnp.float32, 0.0, 1.0)
    return jnp.stack([density, motion[0], motion[1], motion[2], pressure, metals]).astype(jnp.float32)


def draw_owner(key, part):
    key = jax.random.fold_in(key, 9)
    count = GPX * GPY
    blocks = GXT // GPX
    columns = NYG // GPY
    first, second = jax.random.split(key)
    offsets = jax.vmap(lambda sub: jax.random.permutation(sub, blocks)[:count])(jax.random.split(first, columns))
    slot_perm = jax.vmap(lambda sub: jax.random.permutation(sub, count))(jax.random.split(second, blocks * columns))
    slot_perm = slot_perm.reshape(blocks, columns, count)
    xindex = jnp.arange(GXT, dtype=jnp.int32)[:, None]
    yindex = jnp.arange(NYG, dtype=jnp.int32)[None, :]
    source = xindex // GPX
    column = yindex // GPY
    local = xindex % GPX * GPY + yindex % GPY
    which = slot_perm[source, column, local]
    return ((source + offsets[column, which]) % blocks).astype(jnp.int32)


def setup_inputs(seed: int = 0) -> dict:
    seeds = jax.random.split(jax.random.key(seed), 3)
    fields = draw_fields(jax.random.fold_in(seeds[2], 71), 0)
    owner = draw_owner(jax.random.fold_in(seeds[2], 71), 0)
    return {"fields": fields, "owner": owner}


gamma_gas = 5.0 / 3.0
courant_factor = 0.4

def window(values, start, stop, along):
    return lax.slice_in_dim(values, start, stop, axis=along)

def face_states(values, along):
    length = values.shape[along]
    middle_a = window(values, 1, length - 2, along)
    middle_b = window(values, 2, length - 1, along)
    outer_a = window(values, 0, length - 3, along)
    outer_b = window(values, 3, length, along)
    interface = 7.0 / 12.0 * (middle_a + middle_b) - 1.0 / 12.0 * (outer_a + outer_b)
    interface = jnp.clip(interface, jnp.minimum(middle_a, middle_b), jnp.maximum(middle_a, middle_b))
    center = window(values, 2, length - 2, along)
    left_gap = window(interface, 0, length - 4, along) - center
    right_gap = window(interface, 1, length - 3, along) - center
    right_cut = jnp.clip(right_gap, jnp.minimum(0.0, -2.0 * left_gap), jnp.maximum(0.0, -2.0 * left_gap))
    left_cut = jnp.clip(left_gap, jnp.minimum(0.0, -2.0 * right_gap), jnp.maximum(0.0, -2.0 * right_gap))
    from_left = window(center, 0, length - 5, along) + window(right_cut, 0, length - 5, along)
    from_right = window(center, 1, length - 4, along) + window(left_cut, 1, length - 4, along)
    return (from_left, from_right)

def conserved(density, x_vel, y_vel, z_vel, pressure, metals):
    kinetic = 0.5 * density * (x_vel * x_vel + y_vel * y_vel + z_vel * z_vel)
    energy = pressure / (gamma_gas - 1.0) + kinetic
    return [density, density * x_vel, density * y_vel, density * z_vel, energy, density * metals]

def fluxes(density, x_vel, y_vel, z_vel, pressure, metals):
    momentum = density * x_vel
    energy = pressure / (gamma_gas - 1.0) + 0.5 * density * (x_vel * x_vel + y_vel * y_vel + z_vel * z_vel)
    return [momentum, momentum * x_vel + pressure, momentum * y_vel, momentum * z_vel, x_vel * (energy + pressure), momentum * metals]

def x_update(primitive, along, courant):
    states = [face_states(values, along) for values in primitive]
    left_side = [state[0] for state in states]
    right_side = [state[1] for state in states]
    left_sound = jnp.sqrt(gamma_gas * left_side[4] / left_side[0])
    right_sound = jnp.sqrt(gamma_gas * right_side[4] / right_side[0])
    slowest = jnp.minimum(jnp.minimum(left_side[1] - left_sound, right_side[1] - right_sound), 0.0)
    fastest = jnp.maximum(jnp.maximum(left_side[1] + left_sound, right_side[1] + right_sound), 0.0)
    spread = fastest - slowest
    one_cons = conserved(*left_side)
    two_cons = conserved(*right_side)
    one_flux = fluxes(*left_side)
    two_flux = fluxes(*right_side)
    total = [(fastest * lhs_f - slowest * rhs_f + slowest * fastest * (rhs_c - lhs_c)) / spread for lhs_f, rhs_f, lhs_c, rhs_c in zip(one_flux, two_flux, one_cons, two_cons)]
    length = primitive[0].shape[along]
    inner = length - 6
    state = conserved(*[window(values, 3, length - 3, along) for values in primitive])
    return [current - courant * (window(net_flow, 1, inner + 1, along) - window(net_flow, 0, inner, along)) for current, net_flow in zip(state, total)]

def reference(fields, owner):
    fastest = jnp.max(jnp.abs(fields[1]) + jnp.sqrt(gamma_gas * fields[4] / fields[0]))
    courant = courant_factor / fastest
    count = GXT * GPY

    def column(index):
        block = lax.dynamic_slice_in_dim(fields, index * GPY, GPY, axis=2)
        padded = jnp.concatenate([block[:, NX - 3:], block, block[:, :3]], axis=1)
        updated = jnp.stack(x_update([padded[field] for field in range(FIELDS)], 0, courant))
        grids = updated.reshape(FIELDS, GXT, CELLS, GPY, PLANE).transpose(1, 3, 0, 2, 4)
        grids = grids.reshape(count, FIELDS, CELLS, PLANE)
        targets = lax.dynamic_slice_in_dim(owner, index * GPY, GPY, axis=1).reshape(count)
        serial = jnp.arange(count, dtype=jnp.int32)
        sources = serial // GPY // GPX
        order = jnp.argsort(targets * N_GX + sources, stable=True).astype(jnp.int32)
        numbers = (serial // GPY * NYG + index * GPY + serial % GPY).astype(jnp.int32)
        return (grids[order], numbers[order])
    owned, owned_id = lax.map(column, jnp.arange(N_GY, dtype=jnp.int32))
    return (owned, owned_id)
```

```python
import functools

import jax
import jax.numpy as jnp
from jax import lax
from jax.experimental import pallas as pl
from jax.experimental.pallas import tpu as pltpu
from jax.sharding import PartitionSpec as P

CELLS = 32
HALO = 3
LANES = 128
MESH = pl.DeviceIdType.MESH

gamma_gas = 5.0 / 3.0
courant_factor = 0.4

ORDER = (
    (0, 1), (0, 3), (1, 0), (3, 0), (2, 2), (1, 1), (3, 3), (1, 3),
    (3, 1), (0, 2), (2, 0), (1, 2), (3, 2), (2, 1), (2, 3),
)
CODE_Z = sum(dz * 4**k for k, (dz, _) in enumerate(ORDER))
CODE_X = sum(dx * 4**k for k, (_, dx) in enumerate(ORDER))


def peer(me, k, side=4):
    z, x = me // side, me % side
    dz = (CODE_Z // 4**k) % 4 if isinstance(k, int) else lax.shift_right_logical(jnp.int32(CODE_Z), 2 * k) % 4
    dx = (CODE_X // 4**k) % 4 if isinstance(k, int) else lax.shift_right_logical(jnp.int32(CODE_X), 2 * k) % 4
    to = (z + dz) % side * side + (x + dx) % side
    source = (z + side - dz) % side * side + (x + side - dx) % side
    return to, source


def clip(value, low, high):
    return jnp.minimum(jnp.maximum(value, low), high)


def edge_value(far_a, near_a, near_b, far_b):
    value = 7.0 / 12.0 * (near_a + near_b) - 1.0 / 12.0 * (far_a + far_b)
    return clip(value, jnp.minimum(near_a, near_b), jnp.maximum(near_a, near_b))


def cell_states(center, left_edge, right_edge):
    left_gap = left_edge - center
    right_gap = right_edge - center
    left_lim = -2.0 * left_gap
    right_lim = -2.0 * right_gap
    right_cut = clip(right_gap, jnp.minimum(0.0, left_lim), jnp.maximum(0.0, left_lim))
    left_cut = clip(left_gap, jnp.minimum(0.0, right_lim), jnp.maximum(0.0, right_lim))
    return center + left_cut, center + right_cut


def conserved(rho, u, v, w, p, met):
    energy = p / (gamma_gas - 1.0) + 0.5 * rho * (u * u + v * v + w * w)
    return [rho, rho * u, rho * v, rho * w, energy, rho * met]


def flux_of(u, p, cons):
    momentum = cons[1]
    return [
        momentum,
        momentum * u + p,
        u * cons[2],
        u * cons[3],
        u * (cons[4] + p),
        u * cons[5],
    ]


def interface_flux(left, right):
    left_sound = jnp.sqrt(gamma_gas * left[4] / left[0])
    right_sound = jnp.sqrt(gamma_gas * right[4] / right[0])
    slow = jnp.minimum(jnp.minimum(left[1] - left_sound, right[1] - right_sound), 0.0)
    fast = jnp.maximum(jnp.maximum(left[1] + left_sound, right[1] + right_sound), 0.0)
    scale = 1.0 / (fast - slow)
    fast_s, slow_s, both_s = fast * scale, slow * scale, slow * fast * scale
    left_cons, right_cons = conserved(*left), conserved(*right)
    left_flux = flux_of(left[1], left[4], left_cons)
    right_flux = flux_of(right[1], right[4], right_cons)
    return [
        fast_s * lf - slow_s * rf + both_s * (rc - lc)
        for lf, rf, lc, rc in zip(left_flux, right_flux, left_cons, right_cons)
    ]


def sweep_kernel(
    dims, owner_ref, fields_ref, grids_ref, ids_ref,
    prim, cons_s, diff_s, send_buf, top_mine, top_x, top_y, id_send,
    load_sem, halo_send, halo_recv, topx_send, topx_recv, topy_send, topy_recv,
    id_ssem, id_rsem, id_own, out_send, out_recv, own_sem,
):
    ngx, ngy, width, gpy, chunks = dims
    nfield = 6
    others = ngx - 1
    halves = width // CELLS
    me = lax.axis_index("gx")
    col = lax.axis_index("gy")
    right, left = (me + 1) % ngx, (me + ngx - 1) % ngx

    def load(q):
        return pltpu.make_async_copy(fields_ref.at[q], prim.at[q, pl.ds(HALO, width)], load_sem.at[q])

    for q in (0, 4, 1, 2, 3, 5):
        load(q).start()

    barrier = pltpu.get_barrier_semaphore()

    def greet_x(k, carry):
        to, _ = peer(me, k)
        pl.semaphore_signal(barrier, inc=1, device_id=(to, col), device_id_type=MESH)
        return carry

    def greet_y(k, carry):
        pl.semaphore_signal(barrier, inc=1, device_id=(me, (col + 1 + k) % ngy), device_id_type=MESH)
        return carry

    lax.fori_loop(0, others, greet_x, 0)
    lax.fori_loop(0, ngy - 1, greet_y, 0)
    pl.semaphore_wait(barrier, others + ngy - 1)

    def lanes(c):
        start = c * LANES
        return pl.ds(start if isinstance(c, int) else pl.multiple_of(start, LANES), LANES)

    def halo_copies(c):
        up = pltpu.make_async_remote_copy(
            src_ref=fields_ref.at[:, pl.ds(width - HALO, HALO), :, lanes(c)],
            dst_ref=prim.at[:, pl.ds(0, HALO), :, lanes(c)],
            send_sem=halo_send.at[0, c], recv_sem=halo_recv.at[0, c],
            device_id=(right, col), device_id_type=MESH,
        )
        down = pltpu.make_async_remote_copy(
            src_ref=fields_ref.at[:, pl.ds(0, HALO), :, lanes(c)],
            dst_ref=prim.at[:, pl.ds(width + HALO, HALO), :, lanes(c)],
            send_sem=halo_send.at[1, c], recv_sem=halo_recv.at[1, c],
            device_id=(left, col), device_id_type=MESH,
        )
        return up, down

    def send_halo(c, carry):
        for copy in halo_copies(c):
            copy.start()
        return carry

    lax.fori_loop(0, chunks, send_halo, 0)

    for q in (0, 4, 1):
        load(q).wait()

    def speed(x, top):
        for c in range(chunks):
            at = (HALO + x, slice(None), pl.ds(c * LANES, LANES))
            sound = jnp.sqrt(gamma_gas * prim[(4,) + at] / prim[(0,) + at])
            top = jnp.maximum(top, jnp.abs(prim[(1,) + at]) + sound)
        return top

    top_mine[0] = lax.fori_loop(0, width, speed, jnp.zeros((8, LANES), jnp.float32))

    def topx_copy(k):
        to, source = peer(me, k)
        return pltpu.make_async_remote_copy(
            src_ref=top_mine.at[0], dst_ref=top_x.at[k],
            send_sem=topx_send.at[k], recv_sem=topx_recv.at[k],
            device_id=(to, col), device_id_type=MESH,
        )

    def topy_copy(k):
        return pltpu.make_async_remote_copy(
            src_ref=top_mine.at[1], dst_ref=top_y.at[k],
            send_sem=topy_send.at[k], recv_sem=topy_recv.at[k],
            device_id=(me, (col + 1 + k) % ngy), device_id_type=MESH,
        )

    def start(copy):
        def step(k, carry):
            copy(k).start()
            return carry
        return step

    def arrived(copy):
        def step(k, carry):
            copy(k).wait_recv()
            return carry
        return step

    def left_here(copy):
        def step(k, carry):
            copy(k).wait_send()
            return carry
        return step

    lax.fori_loop(0, others, start(topx_copy), 0)
    for q in (2, 3, 5):
        load(q).wait()

    def sweep(c, half):
        first = HALO + half * CELLS

        def q_at(j):
            return [prim[q, j, :, lanes(c)] for q in range(nfield)]

        def edges(j):
            return [edge_value(*qs) for qs in zip(q_at(j - 1), q_at(j), q_at(j + 1), q_at(j + 2))]

        def advance(e, edge, from_left):
            after = edges(e + 1)
            pairs = [cell_states(*vals) for vals in zip(q_at(e + 1), edge, after)]
            flow = interface_flux(from_left, [pair[0] for pair in pairs])
            return after, [pair[1] for pair in pairs], flow

        before, edge = edges(first - 2), edges(first - 1)
        from_left = [cell_states(*vals)[1] for vals in zip(q_at(first - 1), before, edge)]
        edge, from_left, flow = advance(first - 1, edge, from_left)

        def step(i, carry):
            edge, from_left, flow = carry
            e = first + i
            edge, from_left, after = advance(e, edge, from_left)
            rows = pl.ds(pl.multiple_of((half * CELLS + i) * gpy, gpy), gpy)
            for q, value in enumerate(conserved(*q_at(e))):
                cons_s[q, rows, :] = value
            for q in range(nfield):
                diff_s[q, rows, :] = after[q] - flow[q]
            return edge, from_left, after

        lax.fori_loop(0, CELLS, step, (edge, from_left, flow))

    def picked(to):
        number = jnp.int32(0)
        for half in range(halves):
            for b in range(gpy):
                number = jnp.where(owner_ref[half, b] == to, half * gpy + b, number)
        return number

    def extract(c, slot, to, courant):
        number = picked(to)
        base = number // gpy * (CELLS * gpy) + number % gpy
        for t in range(CELLS // 8):
            rows = pl.ds(base + t * 8 * gpy, 8, stride=gpy)
            for q in range(nfield):
                send_buf[slot, q, pl.ds(t * 8, 8), lanes(c)] = cons_s[q, rows, :] - courant * diff_s[q, rows, :]

    def out_copy(c, k):
        to, source = peer(me, k)
        return pltpu.make_async_remote_copy(
            src_ref=send_buf.at[k, :, :, lanes(c)], dst_ref=grids_ref.at[me, :, :, lanes(c)],
            send_sem=out_send.at[c, k], recv_sem=out_recv.at[c, k],
            device_id=(to, col), device_id_type=MESH,
        )

    def own_copy(c):
        return pltpu.make_async_copy(
            send_buf.at[others, :, :, lanes(c)], grids_ref.at[me, :, :, lanes(c)], own_sem.at[c]
        )

    def ship(c, courant):
        def step(k, carry):
            to, _ = peer(me, k)
            extract(c, k, to, courant)
            out_copy(c, k).start()
            return carry

        lax.fori_loop(0, others, step, 0)
        extract(c, others, me, courant)
        own_copy(c).start()

    def halo_here(c):
        for copy in halo_copies(c):
            copy.wait_recv()

    halo_here(0)
    sweep(0, 0)
    lax.fori_loop(0, others, arrived(topx_copy), 0)
    top_mine[1] = jnp.maximum(top_mine[0], jnp.max(top_x[...], axis=0))
    lax.fori_loop(0, ngy - 1, start(topy_copy), 0)
    sweep(0, 1)
    lax.fori_loop(0, ngy - 1, arrived(topy_copy), 0)
    fastest = jnp.max(jnp.maximum(top_mine[1], jnp.max(top_y[...], axis=0)), keepdims=True)
    courant = jnp.broadcast_to(courant_factor / fastest, (8, LANES))
    ship(0, courant)

    def grid_number(to):
        number = picked(to)
        return ((me * halves + number // gpy) * ngy + col) * gpy + number % gpy

    def id_copy(k):
        to, source = peer(me, k)
        return pltpu.make_async_remote_copy(
            src_ref=id_send.at[k], dst_ref=ids_ref.at[me],
            send_sem=id_ssem.at[k], recv_sem=id_rsem.at[k],
            device_id=(to, col), device_id_type=MESH,
        )

    def send_id(k, carry):
        to, _ = peer(me, k)
        id_send[k] = jnp.full((8, LANES), grid_number(to), jnp.int32)
        id_copy(k).start()
        return carry

    lax.fori_loop(0, others, send_id, 0)
    id_send[others] = jnp.full((8, LANES), grid_number(me), jnp.int32)
    own_id = pltpu.make_async_copy(id_send.at[others], ids_ref.at[me], id_own)
    own_id.start()

    def chunk(c, carry):
        halo_here(c)
        for half in range(halves):
            sweep(c, half)
        ship(c, courant)
        return carry

    lax.fori_loop(1, chunks, chunk, 0)

    def finish(c, carry):
        for copy in halo_copies(c):
            copy.wait_send()
        own_copy(c).wait()

        def each(k, inner):
            out_copy(c, k).wait()
            return inner

        return lax.fori_loop(0, others, each, carry)

    lax.fori_loop(0, others, left_here(topx_copy), 0)
    lax.fori_loop(0, ngy - 1, left_here(topy_copy), 0)
    own_id.wait()

    def finish_id(k, carry):
        id_copy(k).wait()
        return carry

    lax.fori_loop(0, others, finish_id, 0)
    lax.fori_loop(0, chunks, finish, 0)


def write_kernel(parts, grids_ref, ids_ref, out_ref, out_ids_ref, sem):
    def copy(i):
        return pltpu.make_async_copy(grids_ref.at[i], out_ref.at[0, i], sem.at[i])

    for i in range(parts):
        copy(i).start()
    column = lax.broadcasted_iota(jnp.int32, (1, parts), 1)
    row = jnp.zeros((1, parts), jnp.int32)
    for i in range(parts):
        row = jnp.where(column == i, ids_ref[i, 0:1, 0:parts], row)
    out_ids_ref[...] = row
    for i in range(parts):
        copy(i).wait()


def shards(ngx, ngy, fields, owner):
    nfield, width, gpy, plane = fields.shape
    chunks = plane // LANES
    vmem = pl.BlockSpec(memory_space=pltpu.VMEM)
    anywhere = pl.BlockSpec(memory_space=pl.ANY)
    dma = pltpu.SemaphoreType.DMA
    grids, ids = pl.pallas_call(
        functools.partial(sweep_kernel, (ngx, ngy, width, gpy, chunks)),
        out_shape=(
            pltpu.VMEM((ngx, nfield, CELLS, plane), jnp.float32),
            pltpu.VMEM((ngx, 8, LANES), jnp.int32),
        ),
        in_specs=[pl.BlockSpec(memory_space=pltpu.SMEM), anywhere],
        out_specs=(anywhere, anywhere),
        scratch_shapes=[
            pltpu.VMEM((nfield, width + 2 * HALO, gpy, plane), jnp.float32),
            pltpu.VMEM((nfield, width * gpy, LANES), jnp.float32),
            pltpu.VMEM((nfield, width * gpy, LANES), jnp.float32),
            pltpu.VMEM((ngx, nfield, CELLS, plane), jnp.float32),
            pltpu.VMEM((2, 8, LANES), jnp.float32),
            pltpu.VMEM((ngx - 1, 8, LANES), jnp.float32),
            pltpu.VMEM((ngy - 1, 8, LANES), jnp.float32),
            pltpu.VMEM((ngx, 8, LANES), jnp.int32),
            dma((nfield,)), dma((2, chunks)), dma((2, chunks)),
            dma((ngx - 1,)), dma((ngx - 1,)), dma((ngy - 1,)), dma((ngy - 1,)),
            dma((ngx - 1,)), dma((ngx - 1,)), dma,
            dma((chunks, ngx - 1)), dma((chunks, ngx - 1)), dma((chunks,)),
        ],
        compiler_params=pltpu.CompilerParams(
            collective_id=0, has_side_effects=True, vmem_limit_bytes=36 * 2**20
        ),
        name="sweep_and_send",
    )(owner, fields)
    return pl.pallas_call(
        functools.partial(write_kernel, ngx),
        out_shape=(
            jax.ShapeDtypeStruct((1, ngx, nfield, CELLS, plane), jnp.float32),
            jax.ShapeDtypeStruct((1, ngx), jnp.int32),
        ),
        in_specs=[anywhere, vmem],
        out_specs=(anywhere, vmem),
        scratch_shapes=[dma((ngx,))],
        compiler_params=pltpu.CompilerParams(vmem_limit_bytes=2 * 2**20),
        name="write_owned",
    )(pltpu.with_memory_space_constraint(grids, pltpu.VMEM), ids)


def solution(mesh):
    return jax.shard_map(
        functools.partial(shards, mesh.shape["gx"], mesh.shape["gy"]),
        mesh=mesh,
        in_specs=(P(None, "gx", "gy", None), P("gx", "gy")),
        out_specs=(P("gy", "gx", None, None, None), P("gy", "gx")),
        check_vma=False,
    )
```

```python
import functools

import jax
import jax.numpy as jnp
from jax import lax
from jax.experimental import pallas as pl
from jax.experimental.pallas import tpu as pltpu
from jax.sharding import PartitionSpec as P

CELLS = 32
HALO = 3
LANES = 128
PIECES = 4
MESH = pl.DeviceIdType.MESH

gamma_gas = 5.0 / 3.0
courant_factor = 0.4

ORDER = (
    (0, 1), (0, 3), (1, 0), (3, 0), (2, 2), (1, 1), (3, 3), (1, 3),
    (3, 1), (0, 2), (2, 0), (1, 2), (3, 2), (2, 1), (2, 3),
)
CODE_Z = sum(dz * 4**k for k, (dz, _) in enumerate(ORDER))
CODE_X = sum(dx * 4**k for k, (_, dx) in enumerate(ORDER))


def peer(me, k, side=4):
    z, x = me // side, me % side
    dz = (CODE_Z // 4**k) % 4 if isinstance(k, int) else lax.shift_right_logical(jnp.int32(CODE_Z), 2 * k) % 4
    dx = (CODE_X // 4**k) % 4 if isinstance(k, int) else lax.shift_right_logical(jnp.int32(CODE_X), 2 * k) % 4
    to = (z + dz) % side * side + (x + dx) % side
    source = (z + side - dz) % side * side + (x + side - dx) % side
    return to, source


def clip(value, low, high):
    return jnp.minimum(jnp.maximum(value, low), high)


def edge_value(far_a, near_a, near_b, far_b):
    value = 7.0 / 12.0 * (near_a + near_b) - 1.0 / 12.0 * (far_a + far_b)
    return clip(value, jnp.minimum(near_a, near_b), jnp.maximum(near_a, near_b))


def cell_states(center, left_edge, right_edge):
    left_gap = left_edge - center
    right_gap = right_edge - center
    left_lim = -2.0 * left_gap
    right_lim = -2.0 * right_gap
    right_cut = clip(right_gap, jnp.minimum(0.0, left_lim), jnp.maximum(0.0, left_lim))
    left_cut = clip(left_gap, jnp.minimum(0.0, right_lim), jnp.maximum(0.0, right_lim))
    return center + left_cut, center + right_cut


def conserved(rho, u, v, w, p, met):
    energy = p / (gamma_gas - 1.0) + 0.5 * rho * (u * u + v * v + w * w)
    return [rho, rho * u, rho * v, rho * w, energy, rho * met]


def flux_of(u, p, cons):
    momentum = cons[1]
    return [
        momentum,
        momentum * u + p,
        u * cons[2],
        u * cons[3],
        u * (cons[4] + p),
        u * cons[5],
    ]


def interface_flux(left, right):
    left_sound = jnp.sqrt(gamma_gas * left[4] / left[0])
    right_sound = jnp.sqrt(gamma_gas * right[4] / right[0])
    slow = jnp.minimum(jnp.minimum(left[1] - left_sound, right[1] - right_sound), 0.0)
    fast = jnp.maximum(jnp.maximum(left[1] + left_sound, right[1] + right_sound), 0.0)
    scale = 1.0 / (fast - slow)
    fast_s, slow_s, both_s = fast * scale, slow * scale, slow * fast * scale
    left_cons, right_cons = conserved(*left), conserved(*right)
    left_flux = flux_of(left[1], left[4], left_cons)
    right_flux = flux_of(right[1], right[4], right_cons)
    return [
        fast_s * lf - slow_s * rf + both_s * (rc - lc)
        for lf, rf, lc, rc in zip(left_flux, right_flux, left_cons, right_cons)
    ]


def sweep_kernel(
    dims, owner_ref, fields_ref, grids_ref, ids_ref,
    prim, cons_s, diff_s, send_buf, top_mine, top_x, top_y, id_send,
    load_sem, halo_send, halo_recv, topx_send, topx_recv, topy_send, topy_recv,
    id_ssem, id_rsem, id_own, out_send, out_recv, own_sem,
):
    ngx, ngy, width, gpy, chunks = dims
    nfield = 6
    others = ngx - 1
    halves = width // CELLS
    me = lax.axis_index("gx")
    col = lax.axis_index("gy")
    right, left = (me + 1) % ngx, (me + ngx - 1) % ngx

    part = width // PIECES

    def load(q, i):
        return pltpu.make_async_copy(
            fields_ref.at[q, pl.ds(i * part, part)],
            prim.at[q, pl.ds(HALO + i * part, part)],
            load_sem.at[q, i],
        )

    for group in ((0, 4, 1), (2, 3, 5)):
        for i in range(PIECES):
            for q in group:
                load(q, i).start()

    barrier = pltpu.get_barrier_semaphore()

    def greet_x(k, carry):
        to, _ = peer(me, k)
        pl.semaphore_signal(barrier, inc=1, device_id=(to, col), device_id_type=MESH)
        return carry

    def greet_y(k, carry):
        pl.semaphore_signal(barrier, inc=1, device_id=(me, (col + 1 + k) % ngy), device_id_type=MESH)
        return carry

    lax.fori_loop(0, others, greet_x, 0)
    lax.fori_loop(0, ngy - 1, greet_y, 0)

    def lanes(c):
        start = c * LANES
        return pl.ds(start if isinstance(c, int) else pl.multiple_of(start, LANES), LANES)

    def halo_copies(c):
        up = pltpu.make_async_remote_copy(
            src_ref=fields_ref.at[:, pl.ds(width - HALO, HALO), :, lanes(c)],
            dst_ref=prim.at[:, pl.ds(0, HALO), :, lanes(c)],
            send_sem=halo_send.at[0, c], recv_sem=halo_recv.at[0, c],
            device_id=(right, col), device_id_type=MESH,
        )
        down = pltpu.make_async_remote_copy(
            src_ref=fields_ref.at[:, pl.ds(0, HALO), :, lanes(c)],
            dst_ref=prim.at[:, pl.ds(width + HALO, HALO), :, lanes(c)],
            send_sem=halo_send.at[1, c], recv_sem=halo_recv.at[1, c],
            device_id=(left, col), device_id_type=MESH,
        )
        return up, down

    def send_halo(c, carry):
        for copy in halo_copies(c):
            copy.start()
        return carry


    def speed(x, top):
        for c in range(chunks):
            at = (HALO + x, slice(None), pl.ds(c * LANES, LANES))
            sound = jnp.sqrt(gamma_gas * prim[(4,) + at] / prim[(0,) + at])
            top = jnp.maximum(top, jnp.abs(prim[(1,) + at]) + sound)
        return top

    top = jnp.zeros((8, LANES), jnp.float32)
    for i in range(PIECES):
        for q in (0, 4, 1):
            load(q, i).wait()
        top = lax.fori_loop(i * part, (i + 1) * part, speed, top)
    top_mine[0] = top

    def topx_copy(k):
        to, source = peer(me, k)
        return pltpu.make_async_remote_copy(
            src_ref=top_mine.at[0], dst_ref=top_x.at[k],
            send_sem=topx_send.at[k], recv_sem=topx_recv.at[k],
            device_id=(to, col), device_id_type=MESH,
        )

    def topy_copy(k):
        return pltpu.make_async_remote_copy(
            src_ref=top_mine.at[1], dst_ref=top_y.at[k],
            send_sem=topy_send.at[k], recv_sem=topy_recv.at[k],
            device_id=(me, (col + 1 + k) % ngy), device_id_type=MESH,
        )

    def start(copy):
        def step(k, carry):
            copy(k).start()
            return carry
        return step

    def arrived(copy):
        def step(k, carry):
            copy(k).wait_recv()
            return carry
        return step

    def left_here(copy):
        def step(k, carry):
            copy(k).wait_send()
            return carry
        return step

    pl.semaphore_wait(barrier, others + ngy - 1)
    lax.fori_loop(0, others, start(topx_copy), 0)
    send_halo(0, 0)
    for i in range(PIECES):
        for q in (2, 3, 5):
            load(q, i).wait()

    def sweep(c, half):
        first = HALO + half * CELLS

        def q_at(j):
            return [prim[q, j, :, lanes(c)] for q in range(nfield)]

        def edges(j):
            return [edge_value(*qs) for qs in zip(q_at(j - 1), q_at(j), q_at(j + 1), q_at(j + 2))]

        def advance(e, edge, from_left):
            after = edges(e + 1)
            pairs = [cell_states(*vals) for vals in zip(q_at(e + 1), edge, after)]
            flow = interface_flux(from_left, [pair[0] for pair in pairs])
            return after, [pair[1] for pair in pairs], flow

        before, edge = edges(first - 2), edges(first - 1)
        from_left = [cell_states(*vals)[1] for vals in zip(q_at(first - 1), before, edge)]
        edge, from_left, flow = advance(first - 1, edge, from_left)

        def step(i, carry):
            edge, from_left, flow = carry
            e = first + i
            edge, from_left, after = advance(e, edge, from_left)
            rows = pl.ds(pl.multiple_of((half * CELLS + i) * gpy, gpy), gpy)
            for q, value in enumerate(conserved(*q_at(e))):
                cons_s[q, rows, :] = value
            for q in range(nfield):
                diff_s[q, rows, :] = after[q] - flow[q]
            return edge, from_left, after

        lax.fori_loop(0, CELLS, step, (edge, from_left, flow))

    def picked(to):
        number = jnp.int32(0)
        for half in range(halves):
            for b in range(gpy):
                number = jnp.where(owner_ref[half, b] == to, half * gpy + b, number)
        return number

    def extract(c, slot, to, courant):
        number = picked(to)
        base = number // gpy * (CELLS * gpy) + number % gpy
        for t in range(CELLS // 8):
            rows = pl.ds(base + t * 8 * gpy, 8, stride=gpy)
            for q in range(nfield):
                send_buf[slot, q, pl.ds(t * 8, 8), lanes(c)] = cons_s[q, rows, :] - courant * diff_s[q, rows, :]

    def out_copy(c, k):
        to, source = peer(me, k)
        return pltpu.make_async_remote_copy(
            src_ref=send_buf.at[k, :, :, lanes(c)], dst_ref=grids_ref.at[me, :, :, lanes(c)],
            send_sem=out_send.at[c, k], recv_sem=out_recv.at[c, k],
            device_id=(to, col), device_id_type=MESH,
        )

    def own_copy(c):
        return pltpu.make_async_copy(
            send_buf.at[others, :, :, lanes(c)], grids_ref.at[me, :, :, lanes(c)], own_sem.at[c]
        )

    def ship(c, courant):
        def step(k, carry):
            to, _ = peer(me, k)
            extract(c, k, to, courant)
            out_copy(c, k).start()
            return carry

        lax.fori_loop(0, others, step, 0)
        extract(c, others, me, courant)
        own_copy(c).start()

    def halo_here(c):
        for copy in halo_copies(c):
            copy.wait_recv()

    lax.fori_loop(0, others, arrived(topx_copy), 0)
    top_mine[1] = jnp.maximum(top_mine[0], jnp.max(top_x[...], axis=0))
    lax.fori_loop(0, ngy - 1, start(topy_copy), 0)
    lax.fori_loop(1, chunks, send_halo, 0)
    halo_here(0)
    for half in range(halves):
        sweep(0, half)
    lax.fori_loop(0, ngy - 1, arrived(topy_copy), 0)
    fastest = jnp.max(jnp.maximum(top_mine[1], jnp.max(top_y[...], axis=0)), keepdims=True)
    courant = jnp.broadcast_to(courant_factor / fastest, (8, LANES))
    ship(0, courant)

    def grid_number(to):
        number = picked(to)
        return ((me * halves + number // gpy) * ngy + col) * gpy + number % gpy

    def id_copy(k):
        to, source = peer(me, k)
        return pltpu.make_async_remote_copy(
            src_ref=id_send.at[k], dst_ref=ids_ref.at[me],
            send_sem=id_ssem.at[k], recv_sem=id_rsem.at[k],
            device_id=(to, col), device_id_type=MESH,
        )

    def send_id(k, carry):
        to, _ = peer(me, k)
        id_send[k] = jnp.full((8, LANES), grid_number(to), jnp.int32)
        id_copy(k).start()
        return carry

    lax.fori_loop(0, others, send_id, 0)
    id_send[others] = jnp.full((8, LANES), grid_number(me), jnp.int32)
    own_id = pltpu.make_async_copy(id_send.at[others], ids_ref.at[me], id_own)
    own_id.start()

    def chunk(c, carry):
        halo_here(c)
        for half in range(halves):
            sweep(c, half)
        ship(c, courant)
        return carry

    lax.fori_loop(1, chunks, chunk, 0)

    def finish(c, carry):
        for copy in halo_copies(c):
            copy.wait_send()
        own_copy(c).wait()

        def each(k, inner):
            out_copy(c, k).wait()
            return inner

        return lax.fori_loop(0, others, each, carry)

    lax.fori_loop(0, others, left_here(topx_copy), 0)
    lax.fori_loop(0, ngy - 1, left_here(topy_copy), 0)
    own_id.wait()

    def finish_id(k, carry):
        id_copy(k).wait()
        return carry

    lax.fori_loop(0, others, finish_id, 0)
    lax.fori_loop(0, chunks, finish, 0)


def write_kernel(parts, grids_ref, ids_ref, out_ref, out_ids_ref, sem):
    def copy(i):
        return pltpu.make_async_copy(grids_ref.at[i], out_ref.at[0, i], sem.at[i])

    for i in range(parts):
        copy(i).start()
    column = lax.broadcasted_iota(jnp.int32, (1, parts), 1)
    row = jnp.zeros((1, parts), jnp.int32)
    for i in range(parts):
        row = jnp.where(column == i, ids_ref[i, 0:1, 0:parts], row)
    out_ids_ref[...] = row
    for i in range(parts):
        copy(i).wait()


def shards(ngx, ngy, fields, owner):
    nfield, width, gpy, plane = fields.shape
    chunks = plane // LANES
    vmem = pl.BlockSpec(memory_space=pltpu.VMEM)
    anywhere = pl.BlockSpec(memory_space=pl.ANY)
    dma = pltpu.SemaphoreType.DMA
    grids, ids = pl.pallas_call(
        functools.partial(sweep_kernel, (ngx, ngy, width, gpy, chunks)),
        out_shape=(
            pltpu.VMEM((ngx, nfield, CELLS, plane), jnp.float32),
            pltpu.VMEM((ngx, 8, LANES), jnp.int32),
        ),
        in_specs=[pl.BlockSpec(memory_space=pltpu.SMEM), anywhere],
        out_specs=(anywhere, anywhere),
        scratch_shapes=[
            pltpu.VMEM((nfield, width + 2 * HALO, gpy, plane), jnp.float32),
            pltpu.VMEM((nfield, width * gpy, LANES), jnp.float32),
            pltpu.VMEM((nfield, width * gpy, LANES), jnp.float32),
            pltpu.VMEM((ngx, nfield, CELLS, plane), jnp.float32),
            pltpu.VMEM((2, 8, LANES), jnp.float32),
            pltpu.VMEM((ngx - 1, 8, LANES), jnp.float32),
            pltpu.VMEM((ngy - 1, 8, LANES), jnp.float32),
            pltpu.VMEM((ngx, 8, LANES), jnp.int32),
            dma((nfield, PIECES)), dma((2, chunks)), dma((2, chunks)),
            dma((ngx - 1,)), dma((ngx - 1,)), dma((ngy - 1,)), dma((ngy - 1,)),
            dma((ngx - 1,)), dma((ngx - 1,)), dma,
            dma((chunks, ngx - 1)), dma((chunks, ngx - 1)), dma((chunks,)),
        ],
        compiler_params=pltpu.CompilerParams(
            collective_id=0, has_side_effects=True, vmem_limit_bytes=36 * 2**20
        ),
        name="sweep_and_send",
    )(owner, fields)
    return pl.pallas_call(
        functools.partial(write_kernel, ngx),
        out_shape=(
            jax.ShapeDtypeStruct((1, ngx, nfield, CELLS, plane), jnp.float32),
            jax.ShapeDtypeStruct((1, ngx), jnp.int32),
        ),
        in_specs=[anywhere, vmem],
        out_specs=(anywhere, vmem),
        scratch_shapes=[dma((ngx,))],
        compiler_params=pltpu.CompilerParams(vmem_limit_bytes=2 * 2**20),
        name="write_owned",
    )(pltpu.with_memory_space_constraint(grids, pltpu.VMEM), ids)


def solution(mesh):
    return jax.shard_map(
        functools.partial(shards, mesh.shape["gx"], mesh.shape["gy"]),
        mesh=mesh,
        in_specs=(P(None, "gx", "gy", None), P("gx", "gy")),
        out_specs=(P("gy", "gx", None, None, None), P("gy", "gx")),
        check_vma=False,
    )
```

```python
import functools

import jax
import jax.numpy as jnp
from jax import lax
from jax.experimental import pallas as pl
from jax.experimental.pallas import tpu as pltpu
from jax.sharding import PartitionSpec as P

CELLS = 32
HALO = 3
LANES = 128
PIECES = 4
MESH = pl.DeviceIdType.MESH

gamma_gas = 5.0 / 3.0
courant_factor = 0.4

ORDER = (
    (0, 1), (0, 3), (1, 0), (3, 0), (2, 2), (1, 1), (3, 3), (1, 3),
    (3, 1), (0, 2), (2, 0), (1, 2), (3, 2), (2, 1), (2, 3),
)
CODE_Z = sum(dz * 4**k for k, (dz, _) in enumerate(ORDER))
CODE_X = sum(dx * 4**k for k, (_, dx) in enumerate(ORDER))


def peer(me, k, side=4):
    z, x = me // side, me % side
    dz = (CODE_Z // 4**k) % 4 if isinstance(k, int) else lax.shift_right_logical(jnp.int32(CODE_Z), 2 * k) % 4
    dx = (CODE_X // 4**k) % 4 if isinstance(k, int) else lax.shift_right_logical(jnp.int32(CODE_X), 2 * k) % 4
    to = (z + dz) % side * side + (x + dx) % side
    source = (z + side - dz) % side * side + (x + side - dx) % side
    return to, source


def clip(value, low, high):
    return jnp.minimum(jnp.maximum(value, low), high)


def edge_value(far_a, near_a, near_b, far_b):
    value = 7.0 / 12.0 * (near_a + near_b) - 1.0 / 12.0 * (far_a + far_b)
    return clip(value, jnp.minimum(near_a, near_b), jnp.maximum(near_a, near_b))


def cell_states(center, left_edge, right_edge):
    left_gap = left_edge - center
    right_gap = right_edge - center
    left_lim = -2.0 * left_gap
    right_lim = -2.0 * right_gap
    right_cut = clip(right_gap, jnp.minimum(0.0, left_lim), jnp.maximum(0.0, left_lim))
    left_cut = clip(left_gap, jnp.minimum(0.0, right_lim), jnp.maximum(0.0, right_lim))
    return center + left_cut, center + right_cut


def conserved(rho, u, v, w, p, met):
    energy = p / (gamma_gas - 1.0) + 0.5 * rho * (u * u + v * v + w * w)
    return [rho, rho * u, rho * v, rho * w, energy, rho * met]


def flux_of(u, p, cons):
    momentum = cons[1]
    return [
        momentum,
        momentum * u + p,
        u * cons[2],
        u * cons[3],
        u * (cons[4] + p),
        u * cons[5],
    ]


def interface_flux(left, right):
    left_sound = jnp.sqrt(gamma_gas * left[4] / left[0])
    right_sound = jnp.sqrt(gamma_gas * right[4] / right[0])
    slow = jnp.minimum(jnp.minimum(left[1] - left_sound, right[1] - right_sound), 0.0)
    fast = jnp.maximum(jnp.maximum(left[1] + left_sound, right[1] + right_sound), 0.0)
    scale = 1.0 / (fast - slow)
    fast_s, slow_s, both_s = fast * scale, slow * scale, slow * fast * scale
    left_cons, right_cons = conserved(*left), conserved(*right)
    left_flux = flux_of(left[1], left[4], left_cons)
    right_flux = flux_of(right[1], right[4], right_cons)
    return [
        fast_s * lf - slow_s * rf + both_s * (rc - lc)
        for lf, rf, lc, rc in zip(left_flux, right_flux, left_cons, right_cons)
    ]


def sweep_kernel(
    dims, owner_hbm, fields_ref, grids_ref, ids_ref,
    owner_ref, prim, cons_s, diff_s, send_buf, top_mine, top_x, top_y, id_send,
    owner_sem, load_sem, halo_send, halo_recv, topx_send, topx_recv, topy_send, topy_recv,
    id_ssem, id_rsem, id_own, out_send, out_recv, own_sem,
):
    ngx, ngy, width, gpy, chunks = dims
    nfield = 6
    others = ngx - 1
    halves = width // CELLS
    me = lax.axis_index("gx")
    col = lax.axis_index("gy")
    right, left = (me + 1) % ngx, (me + ngx - 1) % ngx

    part = width // PIECES

    def load(q, i):
        return pltpu.make_async_copy(
            fields_ref.at[q, pl.ds(i * part, part)],
            prim.at[q, pl.ds(HALO + i * part, part)],
            load_sem.at[q, i],
        )

    for group in ((0, 4, 1), (2, 3, 5)):
        for i in range(PIECES):
            for q in group:
                load(q, i).start()

    table = pltpu.make_async_copy(owner_hbm, owner_ref, owner_sem)
    table.start()

    barrier = pltpu.get_barrier_semaphore()

    def greet_x(k, carry):
        to, _ = peer(me, k)
        pl.semaphore_signal(barrier, inc=1, device_id=(to, col), device_id_type=MESH)
        return carry

    def greet_y(k, carry):
        pl.semaphore_signal(barrier, inc=1, device_id=(me, (col + 1 + k) % ngy), device_id_type=MESH)
        return carry

    lax.fori_loop(0, others, greet_x, 0)
    lax.fori_loop(0, ngy - 1, greet_y, 0)

    def lanes(c):
        start = c * LANES
        return pl.ds(start if isinstance(c, int) else pl.multiple_of(start, LANES), LANES)

    def halo_copies(c):
        up = pltpu.make_async_remote_copy(
            src_ref=fields_ref.at[:, pl.ds(width - HALO, HALO), :, lanes(c)],
            dst_ref=prim.at[:, pl.ds(0, HALO), :, lanes(c)],
            send_sem=halo_send.at[0, c], recv_sem=halo_recv.at[0, c],
            device_id=(right, col), device_id_type=MESH,
        )
        down = pltpu.make_async_remote_copy(
            src_ref=fields_ref.at[:, pl.ds(0, HALO), :, lanes(c)],
            dst_ref=prim.at[:, pl.ds(width + HALO, HALO), :, lanes(c)],
            send_sem=halo_send.at[1, c], recv_sem=halo_recv.at[1, c],
            device_id=(left, col), device_id_type=MESH,
        )
        return up, down

    def send_halo(c, carry):
        for copy in halo_copies(c):
            copy.start()
        return carry


    def speed(x, top):
        for c in range(chunks):
            at = (HALO + x, slice(None), pl.ds(c * LANES, LANES))
            sound = jnp.sqrt(gamma_gas * prim[(4,) + at] / prim[(0,) + at])
            top = jnp.maximum(top, jnp.abs(prim[(1,) + at]) + sound)
        return top

    top = jnp.zeros((8, LANES), jnp.float32)
    for i in range(PIECES):
        for q in (0, 4, 1):
            load(q, i).wait()
        top = lax.fori_loop(i * part, (i + 1) * part, speed, top)
    top_mine[0] = top

    def topx_copy(k):
        to, source = peer(me, k)
        return pltpu.make_async_remote_copy(
            src_ref=top_mine.at[0], dst_ref=top_x.at[k],
            send_sem=topx_send.at[k], recv_sem=topx_recv.at[k],
            device_id=(to, col), device_id_type=MESH,
        )

    def topy_copy(k):
        return pltpu.make_async_remote_copy(
            src_ref=top_mine.at[1], dst_ref=top_y.at[k],
            send_sem=topy_send.at[k], recv_sem=topy_recv.at[k],
            device_id=(me, (col + 1 + k) % ngy), device_id_type=MESH,
        )

    def start(copy):
        def step(k, carry):
            copy(k).start()
            return carry
        return step

    def arrived(copy):
        def step(k, carry):
            copy(k).wait_recv()
            return carry
        return step

    def left_here(copy):
        def step(k, carry):
            copy(k).wait_send()
            return carry
        return step

    pl.semaphore_wait(barrier, others + ngy - 1)
    lax.fori_loop(0, others, start(topx_copy), 0)
    lax.fori_loop(0, 2, send_halo, 0)
    for i in range(PIECES):
        for q in (2, 3, 5):
            load(q, i).wait()

    def sweep(c, half):
        first = HALO + half * CELLS

        def q_at(j):
            return [prim[q, j, :, lanes(c)] for q in range(nfield)]

        def edges(j):
            return [edge_value(*qs) for qs in zip(q_at(j - 1), q_at(j), q_at(j + 1), q_at(j + 2))]

        def advance(e, edge, from_left):
            after = edges(e + 1)
            pairs = [cell_states(*vals) for vals in zip(q_at(e + 1), edge, after)]
            flow = interface_flux(from_left, [pair[0] for pair in pairs])
            return after, [pair[1] for pair in pairs], flow

        before, edge = edges(first - 2), edges(first - 1)
        from_left = [cell_states(*vals)[1] for vals in zip(q_at(first - 1), before, edge)]
        edge, from_left, flow = advance(first - 1, edge, from_left)

        def step(i, carry):
            edge, from_left, flow = carry
            e = first + i
            edge, from_left, after = advance(e, edge, from_left)
            rows = pl.ds(pl.multiple_of((half * CELLS + i) * gpy, gpy), gpy)
            for q, value in enumerate(conserved(*q_at(e))):
                cons_s[q, rows, :] = value
            for q in range(nfield):
                diff_s[q, rows, :] = after[q] - flow[q]
            return edge, from_left, after

        lax.fori_loop(0, CELLS, step, (edge, from_left, flow))

    def picked(to):
        number = jnp.int32(0)
        for half in range(halves):
            for b in range(gpy):
                number = jnp.where(owner_ref[half, b] == to, half * gpy + b, number)
        return number

    def extract(c, slot, to, courant):
        number = picked(to)
        base = number // gpy * (CELLS * gpy) + number % gpy
        for t in range(CELLS // 8):
            rows = pl.ds(base + t * 8 * gpy, 8, stride=gpy)
            for q in range(nfield):
                send_buf[slot, q, pl.ds(t * 8, 8), lanes(c)] = cons_s[q, rows, :] - courant * diff_s[q, rows, :]

    def out_copy(c, k):
        to, source = peer(me, k)
        return pltpu.make_async_remote_copy(
            src_ref=send_buf.at[k, :, :, lanes(c)], dst_ref=grids_ref.at[me, :, :, lanes(c)],
            send_sem=out_send.at[c, k], recv_sem=out_recv.at[c, k],
            device_id=(to, col), device_id_type=MESH,
        )

    def own_copy(c):
        return pltpu.make_async_copy(
            send_buf.at[others, :, :, lanes(c)], grids_ref.at[me, :, :, lanes(c)], own_sem.at[c]
        )

    def ship(c, courant):
        def step(k, carry):
            to, _ = peer(me, k)
            extract(c, k, to, courant)
            out_copy(c, k).start()
            return carry

        lax.fori_loop(0, others, step, 0)
        extract(c, others, me, courant)
        own_copy(c).start()

    def halo_here(c):
        for copy in halo_copies(c):
            copy.wait_recv()

    table.wait()
    lax.fori_loop(0, others, arrived(topx_copy), 0)
    top_mine[1] = jnp.maximum(top_mine[0], jnp.max(top_x[...], axis=0))
    lax.fori_loop(0, ngy - 1, start(topy_copy), 0)
    lax.fori_loop(2, chunks, send_halo, 0)
    halo_here(0)
    for half in range(halves):
        sweep(0, half)
    lax.fori_loop(0, ngy - 1, arrived(topy_copy), 0)
    fastest = jnp.max(jnp.maximum(top_mine[1], jnp.max(top_y[...], axis=0)), keepdims=True)
    courant = jnp.broadcast_to(courant_factor / fastest, (8, LANES))
    ship(0, courant)

    def grid_number(to):
        number = picked(to)
        return ((me * halves + number // gpy) * ngy + col) * gpy + number % gpy

    def id_copy(k):
        to, source = peer(me, k)
        return pltpu.make_async_remote_copy(
            src_ref=id_send.at[k], dst_ref=ids_ref.at[me],
            send_sem=id_ssem.at[k], recv_sem=id_rsem.at[k],
            device_id=(to, col), device_id_type=MESH,
        )

    def send_id(k, carry):
        to, _ = peer(me, k)
        id_send[k] = jnp.full((8, LANES), grid_number(to), jnp.int32)
        id_copy(k).start()
        return carry

    lax.fori_loop(0, others, send_id, 0)
    id_send[others] = jnp.full((8, LANES), grid_number(me), jnp.int32)
    own_id = pltpu.make_async_copy(id_send.at[others], ids_ref.at[me], id_own)
    own_id.start()

    def chunk(c, carry):
        halo_here(c)
        for half in range(halves):
            sweep(c, half)
        ship(c, courant)
        return carry

    lax.fori_loop(1, chunks, chunk, 0)

    def finish(c, carry):
        for copy in halo_copies(c):
            copy.wait_send()
        own_copy(c).wait()

        def each(k, inner):
            out_copy(c, k).wait()
            return inner

        return lax.fori_loop(0, others, each, carry)

    lax.fori_loop(0, others, left_here(topx_copy), 0)
    lax.fori_loop(0, ngy - 1, left_here(topy_copy), 0)
    own_id.wait()

    def finish_id(k, carry):
        id_copy(k).wait()
        return carry

    lax.fori_loop(0, others, finish_id, 0)
    lax.fori_loop(0, chunks, finish, 0)


def write_kernel(parts, grids_ref, ids_ref, out_ref, out_ids_ref, row_ref, sem, row_sem):
    def copy(i):
        return pltpu.make_async_copy(grids_ref.at[i], out_ref.at[0, i], sem.at[i])

    for i in range(parts):
        copy(i).start()
    column = lax.broadcasted_iota(jnp.int32, (1, parts), 1)
    row = jnp.zeros((1, parts), jnp.int32)
    for i in range(parts):
        row = jnp.where(column == i, ids_ref[i, 0:1, 0:parts], row)
    row_ref[...] = row
    ids = pltpu.make_async_copy(row_ref, out_ids_ref, row_sem)
    ids.start()
    ids.wait()
    for i in range(parts):
        copy(i).wait()


def shards(ngx, ngy, fields, owner):
    nfield, width, gpy, plane = fields.shape
    chunks = plane // LANES
    vmem = pl.BlockSpec(memory_space=pltpu.VMEM)
    anywhere = pl.BlockSpec(memory_space=pl.ANY)
    dma = pltpu.SemaphoreType.DMA
    grids, ids = pl.pallas_call(
        functools.partial(sweep_kernel, (ngx, ngy, width, gpy, chunks)),
        out_shape=(
            pltpu.VMEM((ngx, nfield, CELLS, plane), jnp.float32),
            pltpu.VMEM((ngx, 8, LANES), jnp.int32),
        ),
        in_specs=[anywhere, anywhere],
        out_specs=(anywhere, anywhere),
        scratch_shapes=[
            pltpu.SMEM((width // CELLS, gpy), jnp.int32),
            pltpu.VMEM((nfield, width + 2 * HALO, gpy, plane), jnp.float32),
            pltpu.VMEM((nfield, width * gpy, LANES), jnp.float32),
            pltpu.VMEM((nfield, width * gpy, LANES), jnp.float32),
            pltpu.VMEM((ngx, nfield, CELLS, plane), jnp.float32),
            pltpu.VMEM((2, 8, LANES), jnp.float32),
            pltpu.VMEM((ngx - 1, 8, LANES), jnp.float32),
            pltpu.VMEM((ngy - 1, 8, LANES), jnp.float32),
            pltpu.VMEM((ngx, 8, LANES), jnp.int32),
            dma, dma((nfield, PIECES)), dma((2, chunks)), dma((2, chunks)),
            dma((ngx - 1,)), dma((ngx - 1,)), dma((ngy - 1,)), dma((ngy - 1,)),
            dma((ngx - 1,)), dma((ngx - 1,)), dma,
            dma((chunks, ngx - 1)), dma((chunks, ngx - 1)), dma((chunks,)),
        ],
        compiler_params=pltpu.CompilerParams(
            collective_id=0, has_side_effects=True, vmem_limit_bytes=36 * 2**20
        ),
        name="sweep_and_send",
    )(pltpu.with_memory_space_constraint(owner, pltpu.HBM), fields)
    return pl.pallas_call(
        functools.partial(write_kernel, ngx),
        out_shape=(
            jax.ShapeDtypeStruct((1, ngx, nfield, CELLS, plane), jnp.float32),
            jax.ShapeDtypeStruct((1, ngx), jnp.int32),
        ),
        in_specs=[anywhere, vmem],
        out_specs=(anywhere, anywhere),
        scratch_shapes=[pltpu.VMEM((1, ngx), jnp.int32), dma((ngx,)), dma],
        compiler_params=pltpu.CompilerParams(vmem_limit_bytes=2 * 2**20),
        name="write_owned",
    )(pltpu.with_memory_space_constraint(grids, pltpu.VMEM), ids)


def solution(mesh):
    return jax.shard_map(
        functools.partial(shards, mesh.shape["gx"], mesh.shape["gy"]),
        mesh=mesh,
        in_specs=(P(None, "gx", "gy", None), P("gx", "gy")),
        out_specs=(P("gy", "gx", None, None, None), P("gy", "gx")),
        check_vma=False,
    )
```

```python
import functools

import jax
import jax.numpy as jnp
from jax import lax
from jax.experimental import pallas as pl
from jax.experimental.pallas import tpu as pltpu
from jax.sharding import PartitionSpec as P

CELLS = 32
HALO = 3
LANES = 128
PIECES = 4
HALOS = ((0, 1), (1, 1), (2, 2), (4, 4))
MESH = pl.DeviceIdType.MESH

gamma_gas = 5.0 / 3.0
courant_factor = 0.4

ORDER = (
    (0, 1), (0, 3), (1, 0), (3, 0), (2, 2), (1, 1), (3, 3), (1, 3),
    (3, 1), (0, 2), (2, 0), (1, 2), (3, 2), (2, 1), (2, 3),
)
CODE_Z = sum(dz * 4**k for k, (dz, _) in enumerate(ORDER))
CODE_X = sum(dx * 4**k for k, (_, dx) in enumerate(ORDER))


def peer(me, k, side=4):
    z, x = me // side, me % side
    dz = (CODE_Z // 4**k) % 4 if isinstance(k, int) else lax.shift_right_logical(jnp.int32(CODE_Z), 2 * k) % 4
    dx = (CODE_X // 4**k) % 4 if isinstance(k, int) else lax.shift_right_logical(jnp.int32(CODE_X), 2 * k) % 4
    to = (z + dz) % side * side + (x + dx) % side
    source = (z + side - dz) % side * side + (x + side - dx) % side
    return to, source


def clip(value, low, high):
    return jnp.minimum(jnp.maximum(value, low), high)


def edge_value(far_a, near_a, near_b, far_b):
    value = 7.0 / 12.0 * (near_a + near_b) - 1.0 / 12.0 * (far_a + far_b)
    return clip(value, jnp.minimum(near_a, near_b), jnp.maximum(near_a, near_b))


def cell_states(center, left_edge, right_edge):
    left_gap = left_edge - center
    right_gap = right_edge - center
    left_lim = -2.0 * left_gap
    right_lim = -2.0 * right_gap
    right_cut = clip(right_gap, jnp.minimum(0.0, left_lim), jnp.maximum(0.0, left_lim))
    left_cut = clip(left_gap, jnp.minimum(0.0, right_lim), jnp.maximum(0.0, right_lim))
    return center + left_cut, center + right_cut


def conserved(rho, u, v, w, p, met):
    energy = p / (gamma_gas - 1.0) + 0.5 * rho * (u * u + v * v + w * w)
    return [rho, rho * u, rho * v, rho * w, energy, rho * met]


def flux_of(u, p, cons):
    momentum = cons[1]
    return [
        momentum,
        momentum * u + p,
        u * cons[2],
        u * cons[3],
        u * (cons[4] + p),
        u * cons[5],
    ]


def interface_flux(left, right):
    left_sound = jnp.sqrt(gamma_gas * left[4] / left[0])
    right_sound = jnp.sqrt(gamma_gas * right[4] / right[0])
    slow = jnp.minimum(jnp.minimum(left[1] - left_sound, right[1] - right_sound), 0.0)
    fast = jnp.maximum(jnp.maximum(left[1] + left_sound, right[1] + right_sound), 0.0)
    scale = 1.0 / (fast - slow)
    fast_s, slow_s, both_s = fast * scale, slow * scale, slow * fast * scale
    left_cons, right_cons = conserved(*left), conserved(*right)
    left_flux = flux_of(left[1], left[4], left_cons)
    right_flux = flux_of(right[1], right[4], right_cons)
    return [
        fast_s * lf - slow_s * rf + both_s * (rc - lc)
        for lf, rf, lc, rc in zip(left_flux, right_flux, left_cons, right_cons)
    ]


def sweep_kernel(
    dims, owner_hbm, fields_ref, grids_ref, ids_ref,
    owner_ref, prim, cons_s, diff_s, send_buf, top_mine, top_x, top_y, id_send,
    owner_sem, load_sem, halo_send, halo_recv, topx_send, topx_recv, topy_send, topy_recv,
    id_ssem, id_rsem, id_own, out_send, out_recv, own_sem,
):
    ngx, ngy, width, gpy, chunks = dims
    nfield = 6
    others = ngx - 1
    halves = width // CELLS
    me = lax.axis_index("gx")
    col = lax.axis_index("gy")
    right, left = (me + 1) % ngx, (me + ngx - 1) % ngx

    part = width // PIECES

    def load(q, i):
        return pltpu.make_async_copy(
            fields_ref.at[q, pl.ds(i * part, part)],
            prim.at[q, pl.ds(HALO + i * part, part)],
            load_sem.at[q, i],
        )

    for group in ((0, 4, 1), (2, 3, 5)):
        for i in range(PIECES):
            for q in group:
                load(q, i).start()

    table = pltpu.make_async_copy(owner_hbm, owner_ref, owner_sem)
    table.start()

    barrier = pltpu.get_barrier_semaphore()

    def greet_x(k, carry):
        to, _ = peer(me, k)
        pl.semaphore_signal(barrier, inc=1, device_id=(to, col), device_id_type=MESH)
        return carry

    def greet_y(k, carry):
        pl.semaphore_signal(barrier, inc=1, device_id=(me, (col + 1 + k) % ngy), device_id_type=MESH)
        return carry

    lax.fori_loop(0, others, greet_x, 0)
    lax.fori_loop(0, ngy - 1, greet_y, 0)

    def lanes(c):
        start = c * LANES
        return pl.ds(start if isinstance(c, int) else pl.multiple_of(start, LANES), LANES)

    def halo_copies(part):
        start_at, count = HALOS[part]
        at = pl.ds(start_at * LANES, count * LANES)
        up = pltpu.make_async_remote_copy(
            src_ref=fields_ref.at[:, pl.ds(width - HALO, HALO), :, at],
            dst_ref=prim.at[:, pl.ds(0, HALO), :, at],
            send_sem=halo_send.at[0, part], recv_sem=halo_recv.at[0, part],
            device_id=(right, col), device_id_type=MESH,
        )
        down = pltpu.make_async_remote_copy(
            src_ref=fields_ref.at[:, pl.ds(0, HALO), :, at],
            dst_ref=prim.at[:, pl.ds(width + HALO, HALO), :, at],
            send_sem=halo_send.at[1, part], recv_sem=halo_recv.at[1, part],
            device_id=(left, col), device_id_type=MESH,
        )
        return up, down

    def send_halo(part):
        for copy in halo_copies(part):
            copy.start()

    def speed(x, top):
        for c in range(chunks):
            at = (HALO + x, slice(None), pl.ds(c * LANES, LANES))
            sound = jnp.sqrt(gamma_gas * prim[(4,) + at] / prim[(0,) + at])
            top = jnp.maximum(top, jnp.abs(prim[(1,) + at]) + sound)
        return top

    top = jnp.zeros((8, LANES), jnp.float32)
    for i in range(PIECES):
        for q in (0, 4, 1):
            load(q, i).wait()
        top = lax.fori_loop(i * part, (i + 1) * part, speed, top)
    top_mine[0] = jnp.max(top, axis=0, keepdims=True)

    def topx_copy(k):
        to, source = peer(me, k)
        return pltpu.make_async_remote_copy(
            src_ref=top_mine.at[0], dst_ref=top_x.at[k],
            send_sem=topx_send.at[k], recv_sem=topx_recv.at[k],
            device_id=(to, col), device_id_type=MESH,
        )

    def topy_copy(k):
        return pltpu.make_async_remote_copy(
            src_ref=top_mine.at[1], dst_ref=top_y.at[k],
            send_sem=topy_send.at[k], recv_sem=topy_recv.at[k],
            device_id=(me, (col + 1 + k) % ngy), device_id_type=MESH,
        )

    def start(copy):
        def step(k, carry):
            copy(k).start()
            return carry
        return step

    def arrived(copy):
        def step(k, carry):
            copy(k).wait_recv()
            return carry
        return step

    def left_here(copy):
        def step(k, carry):
            copy(k).wait_send()
            return carry
        return step

    pl.semaphore_wait(barrier, others + ngy - 1)
    lax.fori_loop(0, others, start(topx_copy), 0)
    send_halo(0)
    send_halo(1)
    for i in range(PIECES):
        for q in (2, 3, 5):
            load(q, i).wait()

    def sweep(c, half):
        first = HALO + half * CELLS

        def q_at(j):
            return [prim[q, j, :, lanes(c)] for q in range(nfield)]

        def edges(j):
            return [edge_value(*qs) for qs in zip(q_at(j - 1), q_at(j), q_at(j + 1), q_at(j + 2))]

        def advance(e, edge, from_left):
            after = edges(e + 1)
            pairs = [cell_states(*vals) for vals in zip(q_at(e + 1), edge, after)]
            flow = interface_flux(from_left, [pair[0] for pair in pairs])
            return after, [pair[1] for pair in pairs], flow

        before, edge = edges(first - 2), edges(first - 1)
        from_left = [cell_states(*vals)[1] for vals in zip(q_at(first - 1), before, edge)]
        edge, from_left, flow = advance(first - 1, edge, from_left)

        def step(i, carry):
            edge, from_left, flow = carry
            e = first + i
            edge, from_left, after = advance(e, edge, from_left)
            rows = pl.ds(pl.multiple_of((half * CELLS + i) * gpy, gpy), gpy)
            for q, value in enumerate(conserved(*q_at(e))):
                cons_s[q, rows, :] = value
            for q in range(nfield):
                diff_s[q, rows, :] = after[q] - flow[q]
            return edge, from_left, after

        lax.fori_loop(0, CELLS, step, (edge, from_left, flow))

    def picked(to):
        number = jnp.int32(0)
        for half in range(halves):
            for b in range(gpy):
                number = jnp.where(owner_ref[half, b] == to, half * gpy + b, number)
        return number

    def extract(c, slot, to, courant):
        number = picked(to)
        base = number // gpy * (CELLS * gpy) + number % gpy
        for t in range(CELLS // 8):
            rows = pl.ds(base + t * 8 * gpy, 8, stride=gpy)
            for q in range(nfield):
                send_buf[slot, q, pl.ds(t * 8, 8), lanes(c)] = cons_s[q, rows, :] - courant * diff_s[q, rows, :]

    def out_copy(c, k):
        to, source = peer(me, k)
        return pltpu.make_async_remote_copy(
            src_ref=send_buf.at[k, :, :, lanes(c)], dst_ref=grids_ref.at[me, :, :, lanes(c)],
            send_sem=out_send.at[c, k], recv_sem=out_recv.at[c, k],
            device_id=(to, col), device_id_type=MESH,
        )

    def own_copy(c):
        return pltpu.make_async_copy(
            send_buf.at[others, :, :, lanes(c)], grids_ref.at[me, :, :, lanes(c)], own_sem.at[c]
        )

    def ship(c, courant):
        def step(k, carry):
            to, _ = peer(me, k)
            extract(c, k, to, courant)
            out_copy(c, k).start()
            return carry

        lax.fori_loop(0, others, step, 0)
        extract(c, others, me, courant)
        own_copy(c).start()

    def halo_here(part):
        for copy in halo_copies(part):
            copy.wait_recv()

    table.wait()
    lax.fori_loop(0, others, arrived(topx_copy), 0)
    top_mine[1] = jnp.maximum(top_mine[0], jnp.max(top_x[...], axis=0))
    lax.fori_loop(0, ngy - 1, start(topy_copy), 0)
    for part in range(2, len(HALOS)):
        send_halo(part)
    halo_here(0)
    for half in range(halves):
        sweep(0, half)
    lax.fori_loop(0, ngy - 1, arrived(topy_copy), 0)
    fastest = jnp.max(jnp.maximum(top_mine[1], jnp.max(top_y[...], axis=0)), keepdims=True)
    courant = jnp.broadcast_to(courant_factor / fastest, (8, LANES))
    ship(0, courant)

    def grid_number(to):
        number = picked(to)
        return ((me * halves + number // gpy) * ngy + col) * gpy + number % gpy

    def id_copy(k):
        to, source = peer(me, k)
        return pltpu.make_async_remote_copy(
            src_ref=id_send.at[k], dst_ref=ids_ref.at[me],
            send_sem=id_ssem.at[k], recv_sem=id_rsem.at[k],
            device_id=(to, col), device_id_type=MESH,
        )

    def send_id(k, carry):
        to, _ = peer(me, k)
        id_send[k] = jnp.full((8, LANES), grid_number(to), jnp.int32)
        id_copy(k).start()
        return carry

    lax.fori_loop(0, others, send_id, 0)
    id_send[others] = jnp.full((8, LANES), grid_number(me), jnp.int32)
    own_id = pltpu.make_async_copy(id_send.at[others], ids_ref.at[me], id_own)
    own_id.start()

    def chunk(c, carry):
        for part, (start_at, _) in enumerate(HALOS[1:], 1):
            pl.when(c == start_at)(functools.partial(halo_here, part))
        for half in range(halves):
            sweep(c, half)
        ship(c, courant)
        return carry

    lax.fori_loop(1, chunks, chunk, 0)

    def finish(c, carry):
        own_copy(c).wait()

        def each(k, inner):
            out_copy(c, k).wait()
            return inner

        return lax.fori_loop(0, others, each, carry)

    lax.fori_loop(0, others, left_here(topx_copy), 0)
    lax.fori_loop(0, ngy - 1, left_here(topy_copy), 0)
    own_id.wait()

    def finish_id(k, carry):
        id_copy(k).wait()
        return carry

    lax.fori_loop(0, others, finish_id, 0)
    for part in range(len(HALOS)):
        for copy in halo_copies(part):
            copy.wait_send()
    lax.fori_loop(0, chunks, finish, 0)


def write_kernel(parts, grids_ref, ids_ref, out_ref, out_ids_ref, row_ref, sem, row_sem):
    def copy(i):
        return pltpu.make_async_copy(grids_ref.at[i], out_ref.at[0, i], sem.at[i])

    for i in range(parts):
        copy(i).start()
    column = lax.broadcasted_iota(jnp.int32, (1, parts), 1)
    row = jnp.zeros((1, parts), jnp.int32)
    for i in range(parts):
        row = jnp.where(column == i, ids_ref[i, 0:1, 0:parts], row)
    row_ref[...] = row
    ids = pltpu.make_async_copy(row_ref, out_ids_ref, row_sem)
    ids.start()
    ids.wait()
    for i in range(parts):
        copy(i).wait()


def shards(ngx, ngy, fields, owner):
    nfield, width, gpy, plane = fields.shape
    chunks = plane // LANES
    vmem = pl.BlockSpec(memory_space=pltpu.VMEM)
    anywhere = pl.BlockSpec(memory_space=pl.ANY)
    dma = pltpu.SemaphoreType.DMA
    grids, ids = pl.pallas_call(
        functools.partial(sweep_kernel, (ngx, ngy, width, gpy, chunks)),
        out_shape=(
            pltpu.VMEM((ngx, nfield, CELLS, plane), jnp.float32),
            pltpu.VMEM((ngx, 8, LANES), jnp.int32),
        ),
        in_specs=[anywhere, anywhere],
        out_specs=(anywhere, anywhere),
        scratch_shapes=[
            pltpu.SMEM((width // CELLS, gpy), jnp.int32),
            pltpu.VMEM((nfield, width + 2 * HALO, gpy, plane), jnp.float32),
            pltpu.VMEM((nfield, width * gpy, LANES), jnp.float32),
            pltpu.VMEM((nfield, width * gpy, LANES), jnp.float32),
            pltpu.VMEM((ngx, nfield, CELLS, plane), jnp.float32),
            pltpu.VMEM((2, 1, LANES), jnp.float32),
            pltpu.VMEM((ngx - 1, 1, LANES), jnp.float32),
            pltpu.VMEM((ngy - 1, 1, LANES), jnp.float32),
            pltpu.VMEM((ngx, 8, LANES), jnp.int32),
            dma, dma((nfield, PIECES)), dma((2, len(HALOS))), dma((2, len(HALOS))),
            dma((ngx - 1,)), dma((ngx - 1,)), dma((ngy - 1,)), dma((ngy - 1,)),
            dma((ngx - 1,)), dma((ngx - 1,)), dma,
            dma((chunks, ngx - 1)), dma((chunks, ngx - 1)), dma((chunks,)),
        ],
        compiler_params=pltpu.CompilerParams(
            collective_id=0, has_side_effects=True, vmem_limit_bytes=36 * 2**20
        ),
        name="sweep_and_send",
    )(pltpu.with_memory_space_constraint(owner, pltpu.HBM), fields)
    return pl.pallas_call(
        functools.partial(write_kernel, ngx),
        out_shape=(
            jax.ShapeDtypeStruct((1, ngx, nfield, CELLS, plane), jnp.float32),
            jax.ShapeDtypeStruct((1, ngx), jnp.int32),
        ),
        in_specs=[anywhere, vmem],
        out_specs=(anywhere, anywhere),
        scratch_shapes=[pltpu.VMEM((1, ngx), jnp.int32), dma((ngx,)), dma],
        compiler_params=pltpu.CompilerParams(vmem_limit_bytes=2 * 2**20),
        name="write_owned",
    )(pltpu.with_memory_space_constraint(grids, pltpu.VMEM), ids)


def solution(mesh):
    return jax.shard_map(
        functools.partial(shards, mesh.shape["gx"], mesh.shape["gy"]),
        mesh=mesh,
        in_specs=(P(None, "gx", "gy", None), P("gx", "gy")),
        out_specs=(P("gy", "gx", None, None, None), P("gy", "gx")),
        check_vma=False,
    )
```
